512 devices in a mesh: chan: 32 (over z, y_hi), freq: 16 (over y_lo, x, core).
Axes of the slice: x: 4, y: 4 (y_hi: 2, y_lo: 2; y = y_hi * 2 + y_lo), z: 16, core: 2. Of those that a mesh axis runs over, the one named last changes fastest.
Arguments:
- signal: bfloat16 [4096, 131072], P('chan', 'freq'), may hold values from -6 to 6
Outputs:
- cross_spectra: bfloat16 [2, 1024, 32, 4096], P(None, 'freq', None, 'chan')
The draws below stay inside these ranges and needn't reach their ends.
All inputs are finite; a program needn't handle non-finite values.
Results may differ from the reference program's by a relative error of at most 0.01.
Values may be sent and summed in bfloat16 or wider, within the bound.
A program may use at most 64 MiB of HBM per device.

```python
import math
import jax
import jax.numpy as jnp
from jax import lax

L = 2048
CH_DEV = 128
REF_DEV = 1
BINS = 1024
CHANNELS = 4096
SEGS = 64
REFS = 32
N_CHAN = 32


def levels(own_key, shape, cuts, low, high):
    factor_of = 1.0
    for dim, shards_of in cuts:
        draws = jax.random.uniform(jax.random.fold_in(jax.random.fold_in(own_key, 6), dim), (shards_of,), jnp.float32, low / len(cuts), high / len(cuts))
        factor_of = factor_of * jnp.repeat(jnp.exp(draws), shape[dim] // shards_of).reshape((-1,) + (1,) * (len(shape) - 1 - dim))
    return factor_of


def scatter_about(stream_key, extent, scale, limit, pieces=(), held_as=jnp.bfloat16):
    values = jax.random.normal(stream_key, extent, jnp.float32) * scale
    if len(pieces) > 0:
        values = levels(stream_key, extent, pieces, -0.22, 0.18) * values
    return jnp.clip(values, min=-limit, max=limit).astype(held_as)


def setup_inputs(seed: int = 0) -> dict:
    key_of = jax.random.split(jax.random.key(seed), 2)
    signal = scatter_about(key_of[0], (CHANNELS, SEGS * L), 1.0, 6.0, ((0, 32), (1, 16)))
    return {"signal": signal}


def make_window():
    n = jnp.arange(L, dtype=jnp.float32)
    return 0.5 - 0.5 * jnp.cos(2.0 * math.pi * n / L)


def make_table():
    n = jnp.arange(L, dtype=jnp.int32)[:, None]
    k = jnp.arange(BINS, dtype=jnp.int32)[None, :]
    angle = 2.0 * math.pi * ((n * k) % L).astype(jnp.float32) / L
    return jnp.concatenate([jnp.cos(angle), -jnp.sin(angle)], axis=1).astype(jnp.bfloat16)


def transform(block, window, table):
    rows = block.shape[0]
    seg = block.astype(jnp.float32).reshape(rows, SEGS, L)
    seg = seg - jnp.mean(seg, axis=2, keepdims=True)
    windowed = (seg * window).astype(jnp.bfloat16)
    spec = jnp.dot(windowed.reshape(rows * SEGS, L), table, preferred_element_type=jnp.float32)
    return spec.astype(jnp.bfloat16).reshape(rows, SEGS, 2 * BINS)


def reference(signal):
    window = make_window()
    power = jnp.sum(window * window)
    table = make_table()
    blocks = signal.reshape(N_CHAN, CH_DEV, SEGS * L)
    ref_rows = blocks[:, :REF_DEV, :].reshape(REFS, SEGS * L)
    ref_spec = transform(ref_rows, window, table).astype(jnp.float32)
    ref_re = ref_spec[:, :, :BINS]
    ref_im = ref_spec[:, :, BINS:]
    scale = 1.0 / (SEGS * power)

    def one_block(block):
        spec = transform(block, window, table).astype(jnp.float32)
        chan_re = spec[:, :, :BINS]
        chan_im = spec[:, :, BINS:]
        real_part = jnp.einsum("csk,rsk->krc", chan_re, ref_re) + jnp.einsum("csk,rsk->krc", chan_im, ref_im)
        imag_part = jnp.einsum("csk,rsk->krc", chan_im, ref_re) - jnp.einsum("csk,rsk->krc", chan_re, ref_im)
        return (jnp.stack([real_part, imag_part]) * scale).astype(jnp.bfloat16)

    result = lax.map(one_block, blocks)
    return jnp.transpose(result, (1, 2, 3, 0, 4)).reshape(2, BINS, REFS, CHANNELS)
```

```python
import functools

import jax
import jax.numpy as jnp
import ml_dtypes
import numpy as np
from jax import lax
from jax.experimental import pallas as pl
from jax.experimental.pallas import tpu as pltpu
from jax.sharding import PartitionSpec as P

MESH = pl.DeviceIdType.MESH
L = 2048
BINS = 1024
SEG_DEV = 4
CH = 128
REFS = 32
SEGS = 64
Z_OFFSETS = (4, 8, 12, 1, 15, 2, 14)
NT = (((1,), (1,)), ((), ()))


def make_window():
    n = np.arange(L, dtype=np.float64)
    return (0.5 - 0.5 * np.cos(2.0 * np.pi * n / L)).astype(np.float32)


def make_table():
    core, chip, part, group, ri, b = np.ix_(*(np.arange(m) for m in (2, 8, 2, 8, 2, 4)))
    k = ((chip * 2 + core) * 64 + part * 32 + group * 4 + b + 0 * ri).reshape(2, 8, 2, 64)
    second = (ri + 0 * (core + chip + part + group + b)).reshape(2, 8, 2, 64)
    angle = 2.0 * np.pi * np.arange(L, dtype=np.float64) / L
    waves = np.stack([np.cos(angle), -np.sin(angle)]).astype(np.float32).astype(ml_dtypes.bfloat16)
    n = np.arange(L)
    return waves[second[..., None], (k[..., None] * n) % L]


def kernel(
    sig_hbm, tab_hbm, win_ref, out_ref,
    sig, sig2, tab, wnd, sbuf, data, rsend, rrecv, blocks, rf, lhs,
    sig_sem, tab_sem, xs_sem, xr_sem, bs_sem, br_sem, bl_sem,
    rs_sem, rr_sem, ys_sem, yr_sem, zs_sem, zr_sem, ready,
):
    c = lax.axis_index("chan")
    f = lax.axis_index("freq")
    z, yh = c // 2, c % 2
    core, q = f % 2, f // 2
    yl, x = q // 4, q % 4
    cls, za = z % 4, z // 4
    scale = np.float32(1.0 / (SEGS * np.sum(make_window().astype(np.float64) ** 2)))

    def chip(e, i):
        return (yl + i + 1 + e) % 2, (x + i + 2) % 4

    def source(e, i):
        return (yl + i + 1 + e) % 2, (x + 8 - i - 2) % 4

    def freq_of(yx):
        return (yx[0] * 4 + yx[1]) * 2 + core

    def zpeer(o):
        return ((z + o) % 16) * 2 + yh

    load_sig = pltpu.make_async_copy(sig_hbm, sig, sig_sem)
    load_sig.start()
    for d in range(8):
        ty, tx = chip(d // 4, d % 4)
        pltpu.make_async_copy(tab_hbm.at[core, ty * 4 + tx], tab.at[d], tab_sem.at[d]).start()

    barrier = pltpu.get_barrier_semaphore()
    for d in range(8):
        if d != 6:
            pl.semaphore_signal(
                barrier, inc=1, device_id=(c, freq_of(source(d // 4, d % 4))), device_id_type=MESH
            )
    partner = (c, f + 1 - 2 * core)
    ypartner = (z * 2 + 1 - yh, f)
    pl.semaphore_signal(barrier, inc=1, device_id=partner, device_id_type=MESH)
    pl.semaphore_signal(barrier, inc=1, device_id=ypartner, device_id_type=MESH)
    for o in Z_OFFSETS:
        @pl.when(z + o < 16)
        def _():
            pl.semaphore_signal(barrier, inc=1, device_id=(zpeer(o), f), device_id_type=MESH)

    def windowed(h, src, group):
        rows = pl.ds(pl.multiple_of(group * 16, 16), 16)
        for s in range(SEG_DEV):
            seg = src[rows, s * L:(s + 1) * L].astype(jnp.float32)
            mean = jnp.sum(seg, axis=1, keepdims=True) * np.float32(1.0 / L)
            wnd[h, s, rows, :] = ((seg - mean) * win_ref[...]).astype(jnp.bfloat16)

    def transform(h, e, p):
        t = tab[pl.ds(e * 4, 4), p].reshape(256, L)
        w = wnd[h].reshape(SEG_DEV * CH, L)
        spec = lax.dot_general(t, w, NT, preferred_element_type=jnp.float32)
        for i in range(4):
            for sp in range(2):
                pair = [
                    spec[i * 64:(i + 1) * 64, (2 * sp + k) * CH:(2 * sp + k + 1) * CH].reshape(8, 8, CH)
                    for k in range(2)
                ]
                sbuf[h, p, e * 4 + i, sp] = jnp.concatenate(pair, axis=1).astype(jnp.bfloat16)

    def bulk(h, p, e, i):
        return pltpu.make_async_remote_copy(
            src_ref=sbuf.at[h, p, e * 4 + i], dst_ref=data.at[p, q, h],
            send_sem=bs_sem.at[h, p, e * 4 + i], recv_sem=br_sem.at[h, p, e * 4 + i],
            device_id=(c, freq_of(chip(e, i))), device_id_type=MESH,
        )

    def bulk_in(h, p, e, i):
        sy, sx = source(e, i)
        return pltpu.make_async_remote_copy(
            src_ref=sbuf.at[h, p, e * 4 + i], dst_ref=data.at[p, sy * 4 + sx, h],
            send_sem=bs_sem.at[h, p, e * 4 + i], recv_sem=br_sem.at[h, p, e * 4 + i],
            device_id=(c, freq_of(chip(e, i))), device_id_type=MESH,
        )

    def own(h, p):
        return pltpu.make_async_copy(sbuf.at[h, p, 6], data.at[p, q, h], bl_sem.at[h, p])

    def send_bulk(h, p, e):
        for i in range(4):
            if e == 1 and i == 2:
                own(h, p).start()
            else:
                bulk(h, p, e, i).start()

    load_sig.wait()
    lax.fori_loop(0, 8, lambda g, _: (windowed(0, sig, g), 0)[1], 0)
    for d in range(8):
        pltpu.make_async_copy(tab_hbm.at[core, 0], tab.at[d], tab_sem.at[d]).wait()

    def own_chunk(ch, _):
        transform(0, ch % 2, ch // 2)
        return 0

    lax.fori_loop(0, 4, own_chunk, 0)

    early = [jnp.where(z + o >= 16, 1, 0) for o in Z_OFFSETS]
    pl.semaphore_wait(barrier, 9 + sum(early))
    for o in Z_OFFSETS:
        back = Z_OFFSETS.index(16 - o)

        @pl.when(z + o >= 16)
        def _():
            pl.semaphore_signal(ready.at[back], inc=1, device_id=(zpeer(o), f), device_id_type=MESH)

    def wait_ready(o):
        @pl.when(z + o < 16)
        def _():
            pl.semaphore_wait(ready.at[Z_OFFSETS.index(o)], 1)

    cross = [
        pltpu.make_async_remote_copy(
            src_ref=sig.at[rows], dst_ref=sig2.at[rows], send_sem=xs_sem.at[k], recv_sem=xr_sem.at[k],
            device_id=partner, device_id_type=MESH,
        )
        for k, rows in enumerate((pl.ds(0, 16), pl.ds(16, 112)))
    ]
    cross[0].start()
    cross[1].start()

    cross[0].wait_recv()
    windowed(1, sig2, 0)
    rows = [wnd[h, s, 0:16, :].astype(jnp.float32)[0:1] for h in range(2) for s in range(SEG_DEV)]
    wref = jnp.concatenate(rows + [jnp.zeros((8, L), jnp.float32)], axis=0).astype(jnp.bfloat16)
    refs_out = []
    for d in range(0, 8, 2):
        rspec = lax.dot_general(wref, tab[d:d + 2].reshape(256, L), NT, preferred_element_type=jnp.float32)
        rspec = rspec[0:8].astype(jnp.bfloat16).astype(jnp.float32)
        for k in range(2):
            if d + k == 6:
                rrecv[q] = rspec[:, k * 128:(k + 1) * 128]
            else:
                rsend[d + k] = rspec[:, k * 128:(k + 1) * 128]
                yx = chip((d + k) // 4, (d + k) % 4)
                copy = pltpu.make_async_remote_copy(
                    src_ref=rsend.at[d + k], dst_ref=rrecv.at[q],
                    send_sem=rs_sem.at[d + k], recv_sem=rr_sem.at[d + k],
                    device_id=(c, freq_of(yx)), device_id_type=MESH,
                )
                copy.start()
                refs_out.append((d + k, copy))

    for p in range(2):
        for e in range(2):
            send_bulk(0, p, e)

    for d, _ in refs_out:
        sy, sx = source(d // 4, d % 4)
        pltpu.make_async_remote_copy(
            src_ref=rsend.at[d], dst_ref=rrecv.at[sy * 4 + sx], send_sem=rs_sem.at[d], recv_sem=rr_sem.at[d],
            device_id=(c, freq_of(chip(d // 4, d % 4))), device_id_type=MESH,
        ).wait_recv()
    row = lax.broadcasted_iota(jnp.int32, (16, 128), 0)
    lane = lax.broadcasted_iota(jnp.int32, (16, 128), 1)
    diagonal = lane // 8 == row
    for g in range(4):
        a = rrecv[2 * g:2 * g + 2].reshape(16, 128)
        total = jnp.where(diagonal, a, 0.0)
        for d in range(1, 16):
            moved = jnp.where(diagonal, pltpu.roll(a, 8 * d, 1), 0.0)
            total = total + pltpu.roll(moved, 16 - d, 0)
        blocks[cls, za, yh, :, g * 128:(g + 1) * 128] = total.astype(jnp.bfloat16)

    ycopy = pltpu.make_async_remote_copy(
        src_ref=blocks.at[cls, za, yh], dst_ref=blocks.at[cls, za, yh], send_sem=ys_sem, recv_sem=yr_sem,
        device_id=ypartner, device_id_type=MESH,
    )
    ycopy.start()

    cross[1].wait_recv()
    lax.fori_loop(1, 8, lambda g, _: (windowed(1, sig2, g), 0)[1], 0)

    def zcopy(o, src, dst):
        k = Z_OFFSETS.index(o)
        return pltpu.make_async_remote_copy(
            src_ref=src, dst_ref=dst, send_sem=zs_sem.at[k], recv_sem=zr_sem.at[k],
            device_id=(zpeer(o), f), device_id_type=MESH,
        )

    pltpu.make_async_remote_copy(
        src_ref=blocks.at[cls, za, yh], dst_ref=blocks.at[cls, za, 1 - yh], send_sem=ys_sem, recv_sem=yr_sem,
        device_id=ypartner, device_id_type=MESH,
    ).wait_recv()
    sent = []
    for o in (4, 8, 12):
        wait_ready(o)
        copy = zcopy(o, blocks.at[cls, za], blocks.at[cls, za])
        copy.start()
        sent.append(copy)

    for p in range(2):
        for e in range(2):
            transform(1, e, p)
            send_bulk(1, p, e)

    for o in (4, 8, 12):
        zcopy(o, blocks.at[cls, za], blocks.at[cls, (za + 4 - o // 4) % 4]).wait_recv()
    for o in (1, 15, 2, 14):
        wait_ready(o)
        src = {1: blocks.at[cls], 15: blocks.at[cls], 2: blocks.at[cls, 0:2], 14: blocks.at[cls, 2:4]}[o]
        copy = zcopy(o, src, src)
        copy.start()
        sent.append(copy)
    other = (cls + 2) % 4
    for o, got in (
        (1, blocks.at[(cls + 3) % 4]), (15, blocks.at[(cls + 1) % 4]),
        (2, blocks.at[other, 0:2]), (14, blocks.at[other, 2:4]),
    ):
        zcopy(o, got, got).wait_recv()

    for r in range(REFS):
        zr, yr = r // 2, r % 2
        block = blocks[zr % 4, zr // 4, yr].astype(jnp.float32)
        for g in range(4):
            rf[g, r * 16:(r + 1) * 16, :] = block[:, g * 128:(g + 1) * 128]

    wide = lax.broadcasted_iota(jnp.int32, (REFS, 512), 1)

    def build(kg, _):
        re = jnp.concatenate([rf[g, pl.ds(kg, REFS, stride=16), :] for g in range(4)], axis=1)
        im = jnp.where(wide % 8 < 4, -pltpu.roll(re, 508, 1), pltpu.roll(re, 4, 1))
        for b in range(4):
            keep = wide % 4 == b
            lhs[kg, b * 64:b * 64 + 32, :] = jnp.where(keep, re, 0.0).astype(jnp.bfloat16)
            lhs[kg, b * 64 + 32:b * 64 + 64, :] = jnp.where(keep, im, 0.0).astype(jnp.bfloat16)
        return 0

    lax.fori_loop(0, 16, build, 0)

    for p in range(2):
        for h in range(2):
            own(h, p).wait()
            for e in range(2):
                for i in range(4):
                    if not (e == 1 and i == 2):
                        bulk_in(h, p, e, i).wait_recv()

        def products(kg, _):
            right = data[p, :, :, :, kg].reshape(512, CH)
            both = jnp.dot(lhs[p * 8 + kg], right, preferred_element_type=jnp.float32) * scale
            both = both.astype(jnp.bfloat16)
            for b in range(4):
                for ri in range(2):
                    out_ref[ri, (p * 8 + kg) * 4 + b] = both[(b * 2 + ri) * 32:(b * 2 + ri + 1) * 32]
            return 0

        lax.fori_loop(0, 8, products, 0)

    cross[0].wait_send()
    cross[1].wait_send()
    ycopy.wait_send()
    for _, copy in refs_out:
        copy.wait_send()
    for copy in sent:
        copy.wait_send()
    for h in range(2):
        for p in range(2):
            for e in range(2):
                for i in range(4):
                    if not (e == 1 and i == 2):
                        bulk(h, p, e, i).wait_send()


def local(signal, table, window):
    bf16, f32 = jnp.bfloat16, jnp.float32
    dma = pltpu.SemaphoreType.DMA
    return pl.pallas_call(
        kernel,
        out_shape=jax.ShapeDtypeStruct((2, 64, REFS, CH), bf16),
        in_specs=[
            pl.BlockSpec(memory_space=pl.ANY),
            pl.BlockSpec(memory_space=pl.ANY),
            pl.BlockSpec(memory_space=pltpu.VMEM),
        ],
        out_specs=pl.BlockSpec(memory_space=pltpu.VMEM),
        scratch_shapes=[
            pltpu.VMEM((CH, SEG_DEV * L), bf16),
            pltpu.VMEM((CH, SEG_DEV * L), bf16),
            pltpu.VMEM((8, 2, 64, L), bf16),
            pltpu.VMEM((2, SEG_DEV, CH, L), bf16),
            pltpu.VMEM((2, 2, 8, 2, 8, 16, CH), bf16),
            pltpu.VMEM((2, 8, 2, 2, 8, 16, CH), bf16),
            pltpu.VMEM((8, 8, 128), f32),
            pltpu.VMEM((8, 8, 128), f32),
            pltpu.VMEM((4, 4, 2, 16, 512), bf16),
            pltpu.VMEM((4, REFS * 16, 128), f32),
            pltpu.VMEM((16, 256, 512), bf16),
            dma, dma((8,)), dma((2,)), dma((2,)), dma((2, 2, 8)), dma((2, 2, 8)), dma((2, 2)),
            dma((8,)), dma((8,)), dma, dma, dma((7,)), dma((7,)), pltpu.SemaphoreType.REGULAR((7,)),
        ],
        compiler_params=pltpu.CompilerParams(
            collective_id=0, has_side_effects=True, vmem_limit_bytes=52 * 2**20
        ),
        cost_estimate=pl.CostEstimate(flops=5 * 10**9, bytes_accessed=8 * 10**6, transcendentals=0),
        name="cross_spectra",
    )(signal, table, window)


def solution(mesh):
    table = make_table()
    window = make_window()[None, :]

    def whole(signal):
        return local(signal, jnp.asarray(table), jnp.asarray(window))

    return jax.shard_map(
        whole, mesh=mesh, in_specs=(P("chan", "freq"),), out_specs=P(None, "freq", None, "chan"), check_vma=False
    )
```

```python
import functools

import jax
import jax.numpy as jnp
import ml_dtypes
import numpy as np
from jax import lax
from jax.experimental import pallas as pl
from jax.experimental.pallas import tpu as pltpu
from jax.sharding import PartitionSpec as P

MESH = pl.DeviceIdType.MESH
L = 2048
BINS = 1024
SEG_DEV = 4
CH = 128
REFS = 32
SEGS = 64
Z_OFFSETS = (4, 8, 12, 1, 15, 2, 14)
NT = (((1,), (1,)), ((), ()))


def make_window():
    n = np.arange(L, dtype=np.float64)
    return (0.5 - 0.5 * np.cos(2.0 * np.pi * n / L)).astype(np.float32)


def make_table():
    core, chip, part, group, ri, b = np.ix_(*(np.arange(m) for m in (2, 8, 2, 8, 2, 4)))
    k = ((chip * 2 + core) * 64 + part * 32 + group * 4 + b + 0 * ri).reshape(2, 8, 2, 64)
    second = (ri + 0 * (core + chip + part + group + b)).reshape(2, 8, 2, 64)
    angle = 2.0 * np.pi * np.arange(L, dtype=np.float64) / L
    waves = np.stack([np.cos(angle), -np.sin(angle)]).astype(np.float32).astype(ml_dtypes.bfloat16)
    n = np.arange(L)
    return waves[second[..., None], (k[..., None] * n) % L]


def kernel(
    sig_hbm, tab_hbm, win_hbm, out_hbm,
    win_ref, out_ref, sig, sig2, tab, wnd, sbuf, data, rsend, rrecv, blocks, rf, lhs,
    win_sem, sig_sem, tab_sem, xs_sem, xr_sem, bs_sem, br_sem, bl_sem,
    rs_sem, rr_sem, zs_sem, zr_sem, out_sem, ready,
):
    c = lax.axis_index("chan")
    f = lax.axis_index("freq")
    z, yh = c // 2, c % 2
    core, q = f % 2, f // 2
    yl, x = q // 4, q % 4
    cls, za = z % 4, z // 4
    scale = np.float32(1.0 / (SEGS * np.sum(make_window().astype(np.float64) ** 2)))

    def chip(e, i):
        return (yl + i + 1 + e) % 2, (x + i + 2) % 4

    def source(e, i):
        return (yl + i + 1 + e) % 2, (x + 8 - i - 2) % 4

    def freq_of(yx):
        return (yx[0] * 4 + yx[1]) * 2 + core

    def zpeer(o):
        return ((z + o) % 16) * 2 + yh

    load_sig = pltpu.make_async_copy(sig_hbm, sig, sig_sem)
    load_sig.start()
    load_win = pltpu.make_async_copy(win_hbm, win_ref, win_sem)
    load_win.start()
    for d in range(8):
        ty, tx = chip(d // 4, d % 4)
        pltpu.make_async_copy(tab_hbm.at[core, ty * 4 + tx], tab.at[d], tab_sem.at[d]).start()

    barrier = pltpu.get_barrier_semaphore()
    partner = (c, f + 1 - 2 * core)
    other_c = z * 2 + 1 - yh
    for d in range(8):
        sender = freq_of(source(d // 4, d % 4))
        if d != 6:
            pl.semaphore_signal(barrier, inc=1, device_id=(c, sender), device_id_type=MESH)
        pl.semaphore_signal(barrier, inc=1, device_id=(other_c, sender), device_id_type=MESH)
    pl.semaphore_signal(barrier, inc=1, device_id=partner, device_id_type=MESH)
    for o in Z_OFFSETS:
        @pl.when(z + o < 16)
        def _():
            pl.semaphore_signal(barrier, inc=1, device_id=(zpeer(o), f), device_id_type=MESH)

    def windowed(h, src, group):
        rows = pl.ds(pl.multiple_of(group * 16, 16), 16)
        for s in range(SEG_DEV):
            seg = src[rows, s * L:(s + 1) * L].astype(jnp.float32)
            mean = jnp.sum(seg, axis=1, keepdims=True) * np.float32(1.0 / L)
            wnd[h, s, rows, :] = ((seg - mean) * win_ref[...]).astype(jnp.bfloat16)

    def transform(h, e, p):
        t = tab[pl.ds(e * 4, 4), p].reshape(256, L)
        w = wnd[h].reshape(SEG_DEV * CH, L)
        spec = lax.dot_general(t, w, NT, preferred_element_type=jnp.float32)
        for i in range(4):
            for sp in range(2):
                pair = [
                    spec[i * 64:(i + 1) * 64, (2 * sp + k) * CH:(2 * sp + k + 1) * CH].reshape(8, 8, CH)
                    for k in range(2)
                ]
                sbuf[h, p, e * 4 + i, sp] = jnp.concatenate(pair, axis=1).astype(jnp.bfloat16)

    def bulk(h, p, e, i):
        return pltpu.make_async_remote_copy(
            src_ref=sbuf.at[h, p, e * 4 + i], dst_ref=data.at[p, q, h],
            send_sem=bs_sem.at[h, p, e * 4 + i], recv_sem=br_sem.at[h, p, e * 4 + i],
            device_id=(c, freq_of(chip(e, i))), device_id_type=MESH,
        )

    def bulk_in(h, p, e, i):
        sy, sx = source(e, i)
        return pltpu.make_async_remote_copy(
            src_ref=sbuf.at[h, p, e * 4 + i], dst_ref=data.at[p, sy * 4 + sx, h],
            send_sem=bs_sem.at[h, p, e * 4 + i], recv_sem=br_sem.at[h, p, e * 4 + i],
            device_id=(c, freq_of(chip(e, i))), device_id_type=MESH,
        )

    def own(h, p):
        return pltpu.make_async_copy(sbuf.at[h, p, 6], data.at[p, q, h], bl_sem.at[h, p])

    def send_bulk(h, p, e):
        for i in range(4):
            if e == 1 and i == 2:
                own(h, p).start()
            else:
                bulk(h, p, e, i).start()

    load_win.wait()
    load_sig.wait()
    lax.fori_loop(0, 8, lambda g, _: (windowed(0, sig, g), 0)[1], 0)

    early = [jnp.where(z + o >= 16, 1, 0) for o in Z_OFFSETS]
    pl.semaphore_wait(barrier, 16 + sum(early))
    for o in Z_OFFSETS:
        back = Z_OFFSETS.index(16 - o)

        @pl.when(z + o >= 16)
        def _():
            pl.semaphore_signal(ready.at[back], inc=1, device_id=(zpeer(o), f), device_id_type=MESH)

    def wait_ready(o):
        @pl.when(z + o < 16)
        def _():
            pl.semaphore_wait(ready.at[Z_OFFSETS.index(o)], 1)

    cross = [
        pltpu.make_async_remote_copy(
            src_ref=sig.at[rows], dst_ref=sig2.at[rows], send_sem=xs_sem.at[k], recv_sem=xr_sem.at[k],
            device_id=partner, device_id_type=MESH,
        )
        for k, rows in enumerate((pl.ds(0, 16), pl.ds(16, 112)))
    ]
    cross[0].start()
    cross[1].start()

    for d in range(8):
        pltpu.make_async_copy(tab_hbm.at[core, 0], tab.at[d], tab_sem.at[d]).wait()
    lax.fori_loop(0, 2, lambda e, _: (transform(0, e, 0), 0)[1], 0)

    cross[0].wait_recv()
    windowed(1, sig2, 0)
    rows = [wnd[h, s, 0:16, :].astype(jnp.float32)[0:1] for h in range(2) for s in range(SEG_DEV)]
    wref = jnp.concatenate(rows + [jnp.zeros((8, L), jnp.float32)], axis=0).astype(jnp.bfloat16)

    def ref_copy(w, d, slot):
        return pltpu.make_async_remote_copy(
            src_ref=rsend.at[d], dst_ref=rrecv.at[w, slot], send_sem=rs_sem.at[w, d], recv_sem=rr_sem.at[w, d],
            device_id=((c, other_c)[w], freq_of(chip(d // 4, d % 4))), device_id_type=MESH,
        )

    pairs = [(w, d) for d in range(8) for w in range(2) if (w, d) != (0, 6)]
    for d in range(0, 8, 2):
        rspec = lax.dot_general(wref, tab[d:d + 2].reshape(256, L), NT, preferred_element_type=jnp.float32)
        rspec = rspec[0:8].astype(jnp.bfloat16).astype(jnp.float32)
        for k in range(2):
            rsend[d + k] = rspec[:, k * 128:(k + 1) * 128]
            if d + k == 6:
                rrecv[0, q] = rspec[:, k * 128:(k + 1) * 128]
            for w in range(2):
                if (w, d + k) != (0, 6):
                    ref_copy(w, d + k, q).start()

    for e in range(2):
        send_bulk(0, 0, e)
    for e in range(2):
        transform(0, e, 1)
        send_bulk(0, 1, e)

    for w, d in pairs:
        sy, sx = source(d // 4, d % 4)
        ref_copy(w, d, sy * 4 + sx).wait_recv()
    row = lax.broadcasted_iota(jnp.int32, (16, 128), 0)
    lane = lax.broadcasted_iota(jnp.int32, (16, 128), 1)
    diagonal = lane // 8 == row
    for w, y_of in ((0, yh), (1, 1 - yh)):
        for g in range(4):
            a = rrecv[w, 2 * g:2 * g + 2].reshape(16, 128)
            total = jnp.where(diagonal, a, 0.0)
            for d in range(1, 16):
                moved = jnp.where(diagonal, pltpu.roll(a, 8 * d, 1), 0.0)
                total = total + pltpu.roll(moved, 16 - d, 0)
            blocks[cls, za, y_of, :, g * 128:(g + 1) * 128] = total.astype(jnp.bfloat16)

    def zcopy(o, src, dst):
        k = Z_OFFSETS.index(o)
        return pltpu.make_async_remote_copy(
            src_ref=src, dst_ref=dst, send_sem=zs_sem.at[k], recv_sem=zr_sem.at[k],
            device_id=(zpeer(o), f), device_id_type=MESH,
        )

    sent = []
    for o in (4, 12, 8):
        wait_ready(o)
        copy = zcopy(o, blocks.at[cls, za], blocks.at[cls, za])
        copy.start()
        sent.append(copy)

    cross[1].wait_recv()
    lax.fori_loop(1, 8, lambda g, _: (windowed(1, sig2, g), 0)[1], 0)
    for p in range(2):
        for e in range(2):
            transform(1, e, p)
            send_bulk(1, p, e)

    for o in (4, 12, 8):
        zcopy(o, blocks.at[cls, za], blocks.at[cls, (za + 4 - o // 4) % 4]).wait_recv()
    for o in (1, 15, 2, 14):
        wait_ready(o)
        src = {1: blocks.at[cls], 15: blocks.at[cls], 2: blocks.at[cls, 0:2], 14: blocks.at[cls, 2:4]}[o]
        copy = zcopy(o, src, src)
        copy.start()
        sent.append(copy)
    other = (cls + 2) % 4
    for o, got in (
        (1, blocks.at[(cls + 3) % 4]), (15, blocks.at[(cls + 1) % 4]),
        (2, blocks.at[other, 0:2]), (14, blocks.at[other, 2:4]),
    ):
        zcopy(o, got, got).wait_recv()

    for r in range(REFS):
        zr, yr = r // 2, r % 2
        block = blocks[zr % 4, zr // 4, yr].astype(jnp.float32)
        for g in range(4):
            rf[g, r * 16:(r + 1) * 16, :] = block[:, g * 128:(g + 1) * 128]

    wide = lax.broadcasted_iota(jnp.int32, (REFS, 512), 1)

    def build(kg, _):
        re = jnp.concatenate([rf[g, pl.ds(kg, REFS, stride=16), :] for g in range(4)], axis=1)
        im = jnp.where(wide % 8 < 4, -pltpu.roll(re, 508, 1), pltpu.roll(re, 4, 1))
        for b in range(4):
            keep = wide % 4 == b
            lhs[kg, b * 64:b * 64 + 32, :] = jnp.where(keep, re, 0.0).astype(jnp.bfloat16)
            lhs[kg, b * 64 + 32:b * 64 + 64, :] = jnp.where(keep, im, 0.0).astype(jnp.bfloat16)
        return 0

    def store_out(p):
        half = pl.ds(p * 32, 32)
        return pltpu.make_async_copy(out_ref.at[:, half], out_hbm.at[:, half], out_sem.at[p])

    for p in range(2):
        lax.fori_loop(p * 8, p * 8 + 8, build, 0)
        for h in range(2):
            own(h, p).wait()
            for e in range(2):
                for i in range(4):
                    if not (e == 1 and i == 2):
                        bulk_in(h, p, e, i).wait_recv()

        def products(step, _):
            for j in range(4):
                kg = step * 4 + j
                right = data[p, :, :, :, kg].reshape(512, CH)
                both = jnp.dot(lhs[p * 8 + kg], right, preferred_element_type=jnp.float32) * scale
                both = both.astype(jnp.bfloat16)
                for b in range(4):
                    for ri in range(2):
                        out_ref[ri, (p * 8 + kg) * 4 + b] = both[(b * 2 + ri) * 32:(b * 2 + ri + 1) * 32]
            return 0

        lax.fori_loop(0, 2, products, 0)
        store_out(p).start()

    cross[0].wait_send()
    cross[1].wait_send()
    for w, d in pairs:
        ref_copy(w, d, q).wait_send()
    for copy in sent:
        copy.wait_send()
    for h in range(2):
        for p in range(2):
            for e in range(2):
                for i in range(4):
                    if not (e == 1 and i == 2):
                        bulk(h, p, e, i).wait_send()
    store_out(0).wait()
    store_out(1).wait()


def local(signal, table, window):
    bf16, f32 = jnp.bfloat16, jnp.float32
    dma = pltpu.SemaphoreType.DMA
    return pl.pallas_call(
        kernel,
        out_shape=jax.ShapeDtypeStruct((2, 64, REFS, CH), bf16),
        in_specs=[
            pl.BlockSpec(memory_space=pl.ANY),
            pl.BlockSpec(memory_space=pl.ANY),
            pl.BlockSpec(memory_space=pl.ANY),
        ],
        out_specs=pl.BlockSpec(memory_space=pl.ANY),
        scratch_shapes=[
            pltpu.VMEM((1, L), f32),
            pltpu.VMEM((2, 64, REFS, CH), bf16),
            pltpu.VMEM((CH, SEG_DEV * L), bf16),
            pltpu.VMEM((CH, SEG_DEV * L), bf16),
            pltpu.VMEM((8, 2, 64, L), bf16),
            pltpu.VMEM((2, SEG_DEV, CH, L), bf16),
            pltpu.VMEM((2, 2, 8, 2, 8, 16, CH), bf16),
            pltpu.VMEM((2, 8, 2, 2, 8, 16, CH), bf16),
            pltpu.VMEM((8, 8, 128), f32),
            pltpu.VMEM((2, 8, 8, 128), f32),
            pltpu.VMEM((4, 4, 2, 16, 512), bf16),
            pltpu.VMEM((4, REFS * 16, 128), f32),
            pltpu.VMEM((16, 256, 512), bf16),
            dma, dma, dma((8,)), dma((2,)), dma((2,)), dma((2, 2, 8)), dma((2, 2, 8)), dma((2, 2)),
            dma((2, 8)), dma((2, 8)), dma((7,)), dma((7,)), dma((2,)), pltpu.SemaphoreType.REGULAR((7,)),
        ],
        compiler_params=pltpu.CompilerParams(
            collective_id=0, has_side_effects=True, vmem_limit_bytes=52 * 2**20
        ),
        cost_estimate=pl.CostEstimate(flops=5 * 10**9, bytes_accessed=8 * 10**6, transcendentals=0),
        name="cross_spectra",
    )(signal, table, window)


def solution(mesh):
    table = make_table()
    window = make_window()[None, :]

    def whole(signal):
        return local(signal, jnp.asarray(table), jnp.asarray(window))

    return jax.shard_map(
        whole, mesh=mesh, in_specs=(P("chan", "freq"),), out_specs=P(None, "freq", None, "chan"), check_vma=False
    )
```

```python
import functools

import jax
import jax.numpy as jnp
import ml_dtypes
import numpy as np
from jax import lax
from jax.experimental import pallas as pl
from jax.experimental.pallas import tpu as pltpu
from jax.sharding import PartitionSpec as P

MESH = pl.DeviceIdType.MESH
L = 2048
BINS = 1024
SEG_DEV = 4
CH = 128
REFS = 32
SEGS = 64
Z_OFFSETS = (4, 8, 12, 1, 15, 2, 14)
NT = (((1,), (1,)), ((), ()))


def make_window():
    n = np.arange(L, dtype=np.float64)
    return (0.5 - 0.5 * np.cos(2.0 * np.pi * n / L)).astype(np.float32)


def make_table():
    core, chip, part, group, ri, b = np.ix_(*(np.arange(m) for m in (2, 8, 2, 8, 2, 4)))
    k = ((chip * 2 + core) * 64 + part * 32 + group * 4 + b + 0 * ri).reshape(2, 8, 2, 64)
    second = (ri + 0 * (core + chip + part + group + b)).reshape(2, 8, 2, 64)
    angle = 2.0 * np.pi * np.arange(L, dtype=np.float64) / L
    waves = np.stack([np.cos(angle), -np.sin(angle)]).astype(np.float32).astype(ml_dtypes.bfloat16)
    n = np.arange(L)
    return waves[second[..., None], (k[..., None] * n) % L]


def kernel(
    sig_hbm, tab_hbm, win_hbm, out_hbm,
    win_ref, out_ref, sig, sig2, tab, wnd, sbuf, data, rsend, rrecv, blocks, rf, lhs,
    win_sem, sig_sem, tab_sem, cs_sem, cr_sem, bl_sem,
    ys_sem, yr_sem, xs_sem, xr_sem, rs_sem, rr_sem,
    zs_sem, zr_sem, zzs_sem, zzr_sem, out_sem, ready,
):
    c = lax.axis_index("chan")
    f = lax.axis_index("freq")
    z, yh = c // 2, c % 2
    core, q = f % 2, f // 2
    yl, x = q // 4, q % 4
    cls, za = z % 4, z // 4
    scale = np.float32(1.0 / (SEGS * np.sum(make_window().astype(np.float64) ** 2)))

    def chip(e, i):
        return (yl + 1 - e) % 2, (x + i) % 4

    def source(e, i):
        return (yl + 1 - e) % 2, (x + 4 - i) % 4

    def freq_of(yx):
        return (yx[0] * 4 + yx[1]) * 2 + core

    def zpeer(o):
        return ((z + o) % 16) * 2 + yh

    load_sig = pltpu.make_async_copy(sig_hbm, sig, sig_sem)
    load_sig.start()
    load_win = pltpu.make_async_copy(win_hbm, win_ref, win_sem)
    load_win.start()
    for d in range(8):
        ty, tx = chip(d // 4, d % 4)
        pltpu.make_async_copy(tab_hbm.at[core, ty * 4 + tx], tab.at[d], tab_sem.at[d]).start()

    barrier = pltpu.get_barrier_semaphore()
    partner = (c, f + 1 - 2 * core)
    other_c = z * 2 + 1 - yh
    for d in range(8):
        sender = freq_of(source(d // 4, d % 4))
        if d != 4:
            pl.semaphore_signal(barrier, inc=1, device_id=(c, sender), device_id_type=MESH)
        pl.semaphore_signal(barrier, inc=1, device_id=(other_c, sender), device_id_type=MESH)
    pl.semaphore_signal(barrier, inc=1, device_id=partner, device_id_type=MESH)
    for o in Z_OFFSETS:
        @pl.when(z + o < 16)
        def _():
            pl.semaphore_signal(barrier, inc=1, device_id=(zpeer(o), f), device_id_type=MESH)

    def windowed(h, src, group):
        rows = pl.ds(pl.multiple_of(group * 16, 16), 16)
        for s in range(SEG_DEV):
            seg = src[rows, s * L:(s + 1) * L].astype(jnp.float32)
            mean = jnp.sum(seg, axis=1, keepdims=True) * np.float32(1.0 / L)
            wnd[h, s, rows, :] = ((seg - mean) * win_ref[...]).astype(jnp.bfloat16)

    def transform(h, e, p):
        t = tab[pl.ds(e * 4, 4), p].reshape(256, L)
        w = wnd[h].reshape(SEG_DEV * CH, L)
        spec = lax.dot_general(t, w, NT, preferred_element_type=jnp.float32)
        for i in range(4):
            for sp in range(2):
                pair = [
                    spec[i * 64:(i + 1) * 64, (2 * sp + k) * CH:(2 * sp + k + 1) * CH].reshape(8, 8, CH)
                    for k in range(2)
                ]
                sbuf[h, p, e * 4 + i, sp] = jnp.concatenate(pair, axis=1).astype(jnp.bfloat16)

    other_q = (1 - yl) * 4

    def along(i):
        return (c, freq_of((yl, (x + i) % 4)))

    def own(h, p):
        return pltpu.make_async_copy(sbuf.at[h, p, 4], data.at[p, q, h], bl_sem.at[h, p])

    def over_y(h, p, i, slot):
        return pltpu.make_async_remote_copy(
            src_ref=sbuf.at[h, p, i], dst_ref=data.at[p, slot, h],
            send_sem=ys_sem.at[h, p, i], recv_sem=yr_sem.at[h, p, i],
            device_id=(c, freq_of((1 - yl, (x + i) % 4))), device_id_type=MESH,
        )

    def over_x(h, p, i, slot):
        return pltpu.make_async_remote_copy(
            src_ref=sbuf.at[h, p, 4 + i], dst_ref=data.at[p, slot, h],
            send_sem=xs_sem.at[h, p, i], recv_sem=xr_sem.at[h, p, i],
            device_id=along(i), device_id_type=MESH,
        )

    def send(h, p):
        own(h, p).start()
        for i in (2, 1, 3):
            over_y(h, p, i, q).start()
            over_x(h, p, i, q).start()
        over_y(h, p, 0, q).start()

    def receive(h, p):
        own(h, p).wait()
        for i in (1, 2, 3):
            over_x(h, p, i, yl * 4 + (x + 4 - i) % 4).wait_recv()
        for i in range(4):
            over_y(h, p, i, other_q + (x + 4 - i) % 4).wait_recv()

    load_win.wait()
    load_sig.wait()
    lax.fori_loop(0, 8, lambda g, _: (windowed(0, sig, g), 0)[1], 0)

    for d in range(8):
        pltpu.make_async_copy(tab_hbm.at[core, 0], tab.at[d], tab_sem.at[d]).wait()

    def chunk(n, _):
        transform(0, n % 2, n // 2)
        return 0

    ahead = jnp.where((z == 0) & (c + f > 0), 4, 0)
    lax.fori_loop(0, ahead, chunk, 0)

    early = [jnp.where(z + o >= 16, 1, 0) for o in Z_OFFSETS]
    pl.semaphore_wait(barrier, 16 + sum(early))
    for o in Z_OFFSETS:
        back = Z_OFFSETS.index(16 - o)

        @pl.when(z + o >= 16)
        def _():
            pl.semaphore_signal(ready.at[back], inc=1, device_id=(zpeer(o), f), device_id_type=MESH)

    def wait_ready(o):
        @pl.when(z + o < 16)
        def _():
            pl.semaphore_wait(ready.at[Z_OFFSETS.index(o)], 1)

    cross = [
        pltpu.make_async_remote_copy(
            src_ref=sig.at[rows], dst_ref=sig2.at[rows], send_sem=cs_sem.at[k], recv_sem=cr_sem.at[k],
            device_id=partner, device_id_type=MESH,
        )
        for k, rows in enumerate((pl.ds(0, 16), pl.ds(16, 112)))
    ]
    cross[0].start()
    cross[1].start()

    late = z >= 8
    lax.fori_loop(jnp.minimum(ahead, 2), 2, chunk, 0)

    cross[0].wait_recv()
    windowed(1, sig2, 0)
    rows = [wnd[h, s, 0:16, :].astype(jnp.float32)[0:1] for h in range(2) for s in range(SEG_DEV)]
    wref = jnp.concatenate(rows + [jnp.zeros((8, L), jnp.float32)], axis=0).astype(jnp.bfloat16)

    def ref_copy(w, d, slot):
        return pltpu.make_async_remote_copy(
            src_ref=rsend.at[d], dst_ref=rrecv.at[w, slot], send_sem=rs_sem.at[w, d], recv_sem=rr_sem.at[w, d],
            device_id=((c, other_c)[w], freq_of(chip(d // 4, d % 4))), device_id_type=MESH,
        )

    pairs = [(w, d) for d in range(8) for w in range(2) if (w, d) != (0, 4)]
    for d in range(0, 8, 2):
        rspec = lax.dot_general(wref, tab[d:d + 2].reshape(256, L), NT, preferred_element_type=jnp.float32)
        rspec = rspec[0:8].astype(jnp.bfloat16).astype(jnp.float32)
        for k in range(2):
            rsend[d + k] = rspec[:, k * 128:(k + 1) * 128]
            if d + k == 4:
                rrecv[0, q] = rspec[:, k * 128:(k + 1) * 128]
            for w in range(2):
                if (w, d + k) != (0, 4):
                    ref_copy(w, d + k, q).start()

    send(0, 0)
    lax.fori_loop(jnp.maximum(ahead, 2), 4, chunk, 0)
    send(0, 1)

    for w, d in pairs:
        sy, sx = source(d // 4, d % 4)
        ref_copy(w, d, sy * 4 + sx).wait_recv()
    row = lax.broadcasted_iota(jnp.int32, (16, 128), 0)
    lane = lax.broadcasted_iota(jnp.int32, (16, 128), 1)
    diagonal = lane // 8 == row
    for w, y_of in ((0, yh), (1, 1 - yh)):
        for g in range(4):
            a = rrecv[w, 2 * g:2 * g + 2].reshape(16, 128)
            total = jnp.where(diagonal, a, 0.0)
            for d in range(1, 16):
                moved = jnp.where(diagonal, pltpu.roll(a, 8 * d, 1), 0.0)
                total = total + pltpu.roll(moved, 16 - d, 0)
            blocks[cls, za, y_of, :, g * 128:(g + 1) * 128] = total.astype(jnp.bfloat16)

    def far(j, slot):
        return pltpu.make_async_remote_copy(
            src_ref=blocks.at[cls, za], dst_ref=blocks.at[cls, slot], send_sem=zs_sem.at[j], recv_sem=zr_sem.at[j],
            device_id=(zpeer(4 * j), f), device_id_type=MESH,
        )

    def near(o, a, of):
        k = (1, 15, 2, 14).index(o)
        return pltpu.make_async_remote_copy(
            src_ref=blocks.at[of, a], dst_ref=blocks.at[of, a],
            send_sem=zzs_sem.at[k, a], recv_sem=zzr_sem.at[k, a],
            device_id=(zpeer(o), f), device_id_type=MESH,
        )

    def spread():
        for o in (4, 12, 8):
            wait_ready(o)
            far(o // 4, za).start()

    @pl.when(z >= 4)
    def _():
        spread()

    def forward():
        for o in (1, 15, 2, 14):
            wait_ready(o)
        for o in (1, 15):
            near(o, za, cls).start()

        @pl.when(za < 2)
        def _():
            near(2, za, cls).start()

        @pl.when(za >= 2)
        def _():
            near(14, za, cls).start()

        for a in (0, 1, 3, 2):
            @pl.when(za != a)
            def _():
                far((za + 4 - a) % 4, a).wait_recv()
                for o in (1, 15, 2 if a < 2 else 14):
                    near(o, a, cls).start()

    cross[1].wait_recv()
    lax.fori_loop(1, 8, lambda g, _: (windowed(1, sig2, g), 0)[1], 0)
    transform(1, 0, 0)
    transform(1, 1, 0)
    send(1, 0)

    @pl.when(late)
    def _():
        forward()

    transform(1, 0, 1)
    transform(1, 1, 1)
    send(1, 1)

    @pl.when(z < 4)
    def _():
        spread()

    @pl.when(z < 8)
    def _():
        forward()

    for a in range(4):
        near(1, a, (cls + 3) % 4).wait_recv()
        near(15, a, (cls + 1) % 4).wait_recv()
        near(2 if a < 2 else 14, a, (cls + 2) % 4).wait_recv()

    for r in range(REFS):
        zr, yr = r // 2, r % 2
        block = blocks[zr % 4, zr // 4, yr].astype(jnp.float32)
        for g in range(4):
            rf[g, r * 16:(r + 1) * 16, :] = block[:, g * 128:(g + 1) * 128]

    wide = lax.broadcasted_iota(jnp.int32, (REFS, 512), 1)

    def build(kg, _):
        re = jnp.concatenate([rf[g, pl.ds(kg, REFS, stride=16), :] for g in range(4)], axis=1)
        im = jnp.where(wide % 8 < 4, -pltpu.roll(re, 508, 1), pltpu.roll(re, 4, 1))
        for b in range(4):
            keep = wide % 4 == b
            lhs[kg, b * 64:b * 64 + 32, :] = jnp.where(keep, re, 0.0).astype(jnp.bfloat16)
            lhs[kg, b * 64 + 32:b * 64 + 64, :] = jnp.where(keep, im, 0.0).astype(jnp.bfloat16)
        return 0

    def store_out(p):
        half = pl.ds(p * 32, 32)
        return pltpu.make_async_copy(out_ref.at[:, half], out_hbm.at[:, half], out_sem.at[p])

    def multiply(p, kg):
        right = data[p, :, :, :, kg].reshape(512, CH)
        both = jnp.dot(lhs[p * 8 + kg], right, preferred_element_type=jnp.float32) * scale
        both = both.astype(jnp.bfloat16)
        for b in range(4):
            for ri in range(2):
                out_ref[ri, (p * 8 + kg) * 4 + b] = both[(b * 2 + ri) * 32:(b * 2 + ri + 1) * 32]

    def products(p, fused):
        def step(n, _):
            for j in range(4):
                kg = n * 4 + j
                if fused:
                    build(p * 8 + kg, 0)
                multiply(p, kg)
            return 0

        for h in range(2):
            receive(h, p)
        lax.fori_loop(0, 2, step, 0)
        store_out(p).start()

    @pl.when(z < 4)
    def _():
        products(0, True)
        products(1, True)

    @pl.when(z >= 4)
    def _():
        lax.fori_loop(0, 16, build, 0)
        products(0, False)
        products(1, False)

    cross[0].wait_send()
    cross[1].wait_send()
    for w, d in pairs:
        ref_copy(w, d, q).wait_send()
    for j in range(1, 4):
        far(j, za).wait_send()
    for a in range(4):
        for o in (1, 15, 2 if a < 2 else 14):
            near(o, a, cls).wait_send()
    for h in range(2):
        for p in range(2):
            for i in range(4):
                over_y(h, p, i, q).wait_send()
            for i in range(1, 4):
                over_x(h, p, i, q).wait_send()
    store_out(0).wait()
    store_out(1).wait()


def local(signal, table, window):
    bf16, f32 = jnp.bfloat16, jnp.float32
    dma = pltpu.SemaphoreType.DMA
    return pl.pallas_call(
        kernel,
        out_shape=jax.ShapeDtypeStruct((2, 64, REFS, CH), bf16),
        in_specs=[
            pl.BlockSpec(memory_space=pl.ANY),
            pl.BlockSpec(memory_space=pl.ANY),
            pl.BlockSpec(memory_space=pl.ANY),
        ],
        out_specs=pl.BlockSpec(memory_space=pl.ANY),
        scratch_shapes=[
            pltpu.VMEM((1, L), f32),
            pltpu.VMEM((2, 64, REFS, CH), bf16),
            pltpu.VMEM((CH, SEG_DEV * L), bf16),
            pltpu.VMEM((CH, SEG_DEV * L), bf16),
            pltpu.VMEM((8, 2, 64, L), bf16),
            pltpu.VMEM((2, SEG_DEV, CH, L), bf16),
            pltpu.VMEM((2, 2, 8, 2, 8, 16, CH), bf16),
            pltpu.VMEM((2, 8, 2, 2, 8, 16, CH), bf16),
            pltpu.VMEM((8, 8, 128), f32),
            pltpu.VMEM((2, 8, 8, 128), f32),
            pltpu.VMEM((4, 4, 2, 16, 512), bf16),
            pltpu.VMEM((4, REFS * 16, 128), f32),
            pltpu.VMEM((16, 256, 512), bf16),
            dma, dma, dma((8,)), dma((2,)), dma((2,)), dma((2, 2)),
            *[dma((2, 2, 4)) for _ in range(4)], dma((2, 8)), dma((2, 8)),
            dma((4,)), dma((4,)), dma((4, 4)), dma((4, 4)), dma((2,)), pltpu.SemaphoreType.REGULAR((7,)),
        ],
        compiler_params=pltpu.CompilerParams(
            collective_id=0, has_side_effects=True, vmem_limit_bytes=52 * 2**20
        ),
        cost_estimate=pl.CostEstimate(flops=5 * 10**9, bytes_accessed=8 * 10**6, transcendentals=0),
        name="cross_spectra",
    )(signal, table, window)


def solution(mesh):
    table = make_table()
    window = make_window()[None, :]

    def whole(signal):
        return local(signal, jnp.asarray(table), jnp.asarray(window))

    return jax.shard_map(
        whole, mesh=mesh, in_specs=(P("chan", "freq"),), out_specs=P(None, "freq", None, "chan"), check_vma=False
    )
```

```python
import functools

import jax
import jax.numpy as jnp
import ml_dtypes
import numpy as np
from jax import lax
from jax.experimental import pallas as pl
from jax.experimental.pallas import tpu as pltpu
from jax.sharding import PartitionSpec as P

MESH = pl.DeviceIdType.MESH
L = 2048
BINS = 1024
SEG_DEV = 4
CH = 128
REFS = 32
SEGS = 64
Z_OFFSETS = (4, 8, 12, 1, 15, 2, 14)
NT = (((1,), (1,)), ((), ()))


def make_window():
    n = np.arange(L, dtype=np.float64)
    return (0.5 - 0.5 * np.cos(2.0 * np.pi * n / L)).astype(np.float32)


def make_table():
    core, chip, part, group, ri, b = np.ix_(*(np.arange(m) for m in (2, 8, 2, 8, 2, 4)))
    k = ((chip * 2 + core) * 64 + part * 32 + group * 4 + b + 0 * ri).reshape(2, 8, 2, 64)
    second = (ri + 0 * (core + chip + part + group + b)).reshape(2, 8, 2, 64)
    angle = 2.0 * np.pi * np.arange(L, dtype=np.float64) / L
    waves = np.stack([np.cos(angle), -np.sin(angle)]).astype(np.float32).astype(ml_dtypes.bfloat16)
    n = np.arange(L)
    return waves[second[..., None], (k[..., None] * n) % L]


def kernel(
    sig_hbm, tab_hbm, win_hbm, out_hbm,
    win_ref, out_ref, sig, sig2, tab, wnd, sbuf, data, rsend, rrecv, blocks, rf, lhs,
    win_sem, sig_sem, tab_sem, cs_sem, cr_sem, bl_sem,
    ys_sem, yr_sem, xs_sem, xr_sem, rs_sem, rr_sem,
    zs_sem, zr_sem, zzs_sem, zzr_sem, out_sem, ready,
):
    c = lax.axis_index("chan")
    f = lax.axis_index("freq")
    z, yh = c // 2, c % 2
    core, q = f % 2, f // 2
    yl, x = q // 4, q % 4
    cls, za = z % 4, z // 4
    scale = np.float32(1.0 / (SEGS * np.sum(make_window().astype(np.float64) ** 2)))

    def chip(e, i):
        return (yl + 1 - e) % 2, (x + i) % 4

    def source(e, i):
        return (yl + 1 - e) % 2, (x + 4 - i) % 4

    def freq_of(yx):
        return (yx[0] * 4 + yx[1]) * 2 + core

    def zpeer(o):
        return ((z + o) % 16) * 2 + yh

    load_sig = pltpu.make_async_copy(sig_hbm, sig, sig_sem)
    load_sig.start()
    load_win = pltpu.make_async_copy(win_hbm, win_ref, win_sem)
    load_win.start()
    for d in range(8):
        ty, tx = chip(d // 4, d % 4)
        pltpu.make_async_copy(tab_hbm.at[core, ty * 4 + tx], tab.at[d], tab_sem.at[d]).start()

    barrier = pltpu.get_barrier_semaphore()
    partner = (c, f + 1 - 2 * core)
    other_c = z * 2 + 1 - yh
    for d in range(8):
        sender = freq_of(source(d // 4, d % 4))
        if d != 4:
            pl.semaphore_signal(barrier, inc=1, device_id=(c, sender), device_id_type=MESH)
        pl.semaphore_signal(barrier, inc=1, device_id=(other_c, sender), device_id_type=MESH)
    pl.semaphore_signal(barrier, inc=1, device_id=partner, device_id_type=MESH)
    for o in Z_OFFSETS:
        @pl.when(z + o < 16)
        def _():
            pl.semaphore_signal(barrier, inc=1, device_id=(zpeer(o), f), device_id_type=MESH)

    def windowed(h, src, group):
        rows = pl.ds(pl.multiple_of(group * 16, 16), 16)
        for s in range(SEG_DEV):
            seg = src[rows, s * L:(s + 1) * L].astype(jnp.float32)
            mean = jnp.sum(seg, axis=1, keepdims=True) * np.float32(1.0 / L)
            wnd[h, s, rows, :] = ((seg - mean) * win_ref[...]).astype(jnp.bfloat16)

    def transform(h, e, p):
        t = tab[pl.ds(e * 4, 4), p].reshape(256, L)
        w = wnd[h].reshape(SEG_DEV * CH, L)
        spec = lax.dot_general(t, w, NT, preferred_element_type=jnp.float32)
        for i in range(4):
            for sp in range(2):
                pair = [
                    spec[i * 64:(i + 1) * 64, (2 * sp + k) * CH:(2 * sp + k + 1) * CH].reshape(8, 8, CH)
                    for k in range(2)
                ]
                sbuf[h, p, e * 4 + i, sp] = jnp.concatenate(pair, axis=1).astype(jnp.bfloat16)

    other_q = (1 - yl) * 4

    def along(i):
        return (c, freq_of((yl, (x + i) % 4)))

    def own(h, p):
        return pltpu.make_async_copy(sbuf.at[h, p, 4], data.at[p, q, h], bl_sem.at[h, p])

    def over_y(h, p, i, slot):
        return pltpu.make_async_remote_copy(
            src_ref=sbuf.at[h, p, i], dst_ref=data.at[p, slot, h],
            send_sem=ys_sem.at[h, p, i], recv_sem=yr_sem.at[h, p, i],
            device_id=(c, freq_of((1 - yl, (x + i) % 4))), device_id_type=MESH,
        )

    def over_x(h, p, i, slot):
        return pltpu.make_async_remote_copy(
            src_ref=sbuf.at[h, p, 4 + i], dst_ref=data.at[p, slot, h],
            send_sem=xs_sem.at[h, p, i], recv_sem=xr_sem.at[h, p, i],
            device_id=along(i), device_id_type=MESH,
        )

    def send(h, p):
        own(h, p).start()
        for i in (2, 1, 3):
            over_y(h, p, i, q).start()
            over_x(h, p, i, q).start()
        over_y(h, p, 0, q).start()

    def receive(h, p):
        own(h, p).wait()
        for i in (1, 2, 3):
            over_x(h, p, i, yl * 4 + (x + 4 - i) % 4).wait_recv()
        for i in range(4):
            over_y(h, p, i, other_q + (x + 4 - i) % 4).wait_recv()

    load_win.wait()
    load_sig.wait()
    lax.fori_loop(0, 8, lambda g, _: (windowed(0, sig, g), 0)[1], 0)

    for d in range(8):
        pltpu.make_async_copy(tab_hbm.at[core, 0], tab.at[d], tab_sem.at[d]).wait()

    def chunk(n, _):
        transform(0, n % 2, n // 2)
        return 0

    ahead = jnp.where((z == 0) & (c + f > 0), 4, 0)
    lax.fori_loop(0, ahead, chunk, 0)

    early = [jnp.where(z + o >= 16, 1, 0) for o in Z_OFFSETS]
    pl.semaphore_wait(barrier, 16 + sum(early))
    for o in Z_OFFSETS:
        back = Z_OFFSETS.index(16 - o)

        @pl.when(z + o >= 16)
        def _():
            pl.semaphore_signal(ready.at[back], inc=1, device_id=(zpeer(o), f), device_id_type=MESH)

    def wait_ready(o):
        @pl.when(z + o < 16)
        def _():
            pl.semaphore_wait(ready.at[Z_OFFSETS.index(o)], 1)

    cross = [
        pltpu.make_async_remote_copy(
            src_ref=sig.at[rows], dst_ref=sig2.at[rows], send_sem=cs_sem.at[k], recv_sem=cr_sem.at[k],
            device_id=partner, device_id_type=MESH,
        )
        for k, rows in enumerate((pl.ds(0, 16), pl.ds(16, 112)))
    ]
    cross[0].start()
    cross[1].start()

    late = z >= 8
    lax.fori_loop(jnp.minimum(ahead, 2), 2, chunk, 0)

    cross[0].wait_recv()
    windowed(1, sig2, 0)
    rows = [wnd[h, s, 0:16, :].astype(jnp.float32)[0:1] for h in range(2) for s in range(SEG_DEV)]
    wref = jnp.concatenate(rows + [jnp.zeros((8, L), jnp.float32)], axis=0).astype(jnp.bfloat16)

    def ref_copy(w, d, slot):
        return pltpu.make_async_remote_copy(
            src_ref=rsend.at[d], dst_ref=rrecv.at[w, slot], send_sem=rs_sem.at[w, d], recv_sem=rr_sem.at[w, d],
            device_id=((c, other_c)[w], freq_of(chip(d // 4, d % 4))), device_id_type=MESH,
        )

    pairs = [(w, d) for d in range(8) for w in range(2) if (w, d) != (0, 4)]
    for d in range(0, 8, 2):
        rspec = lax.dot_general(wref, tab[d:d + 2].reshape(256, L), NT, preferred_element_type=jnp.float32)
        rspec = rspec[0:8].astype(jnp.bfloat16).astype(jnp.float32)
        for k in range(2):
            rsend[d + k] = rspec[:, k * 128:(k + 1) * 128]
            if d + k == 4:
                rrecv[0, q] = rspec[:, k * 128:(k + 1) * 128]
            for w in range(2):
                if (w, d + k) != (0, 4):
                    ref_copy(w, d + k, q).start()

    send(0, 0)
    lax.fori_loop(jnp.maximum(ahead, 2), 4, chunk, 0)
    send(0, 1)

    for w, d in pairs:
        sy, sx = source(d // 4, d % 4)
        ref_copy(w, d, sy * 4 + sx).wait_recv()
    row = lax.broadcasted_iota(jnp.int32, (16, 128), 0)
    lane = lax.broadcasted_iota(jnp.int32, (16, 128), 1)
    diagonal = lane // 8 == row
    for w, y_of in ((0, yh), (1, 1 - yh)):
        for g in range(4):
            a = rrecv[w, 2 * g:2 * g + 2].reshape(16, 128)
            total = jnp.where(diagonal, a, 0.0)
            for d in range(1, 16):
                moved = jnp.where(diagonal, pltpu.roll(a, 8 * d, 1), 0.0)
                total = total + pltpu.roll(moved, 16 - d, 0)
            blocks[cls, za, y_of, :, g * 128:(g + 1) * 128] = total.astype(jnp.bfloat16)

    def far(j, slot):
        return pltpu.make_async_remote_copy(
            src_ref=blocks.at[cls, za], dst_ref=blocks.at[cls, slot], send_sem=zs_sem.at[j], recv_sem=zr_sem.at[j],
            device_id=(zpeer(4 * j), f), device_id_type=MESH,
        )

    def near(o, a, of):
        k = (1, 15, 2, 14).index(o)
        return pltpu.make_async_remote_copy(
            src_ref=blocks.at[of, a], dst_ref=blocks.at[of, a],
            send_sem=zzs_sem.at[k, a], recv_sem=zzr_sem.at[k, a],
            device_id=(zpeer(o), f), device_id_type=MESH,
        )

    def spread():
        for o in (4, 12, 8):
            wait_ready(o)
            far(o // 4, za).start()

    @pl.when(z >= 4)
    def _():
        spread()

    def forward():
        for o in (1, 15, 2, 14):
            wait_ready(o)
        for o in (1, 15):
            near(o, za, cls).start()

        @pl.when(za < 2)
        def _():
            near(2, za, cls).start()

        @pl.when(za >= 2)
        def _():
            near(14, za, cls).start()

        for a in (0, 1, 3, 2):
            @pl.when(za != a)
            def _():
                far((za + 4 - a) % 4, a).wait_recv()
                for o in (1, 15, 2 if a < 2 else 14):
                    near(o, a, cls).start()

    cross[1].wait_recv()
    lax.fori_loop(1, 8, lambda g, _: (windowed(1, sig2, g), 0)[1], 0)
    transform(1, 0, 0)
    transform(1, 1, 0)
    send(1, 0)

    @pl.when(late)
    def _():
        forward()

    transform(1, 0, 1)
    transform(1, 1, 1)
    send(1, 1)

    @pl.when(z < 4)
    def _():
        spread()

    @pl.when(z < 8)
    def _():
        forward()

    for a in range(4):
        near(1, a, (cls + 3) % 4).wait_recv()
        near(15, a, (cls + 1) % 4).wait_recv()
        near(2 if a < 2 else 14, a, (cls + 2) % 4).wait_recv()

    for r in range(REFS):
        zr, yr = r // 2, r % 2
        block = blocks[zr % 4, zr // 4, yr].astype(jnp.float32)
        for g in range(4):
            rf[g, r * 16:(r + 1) * 16, :] = block[:, g * 128:(g + 1) * 128]

    wide = lax.broadcasted_iota(jnp.int32, (REFS, 512), 1)

    def build(kg, _):
        re = jnp.concatenate([rf[g, pl.ds(kg, REFS, stride=16), :] for g in range(4)], axis=1)
        im = jnp.where(wide % 8 < 4, -pltpu.roll(re, 508, 1), pltpu.roll(re, 4, 1))
        for b in range(4):
            keep = wide % 4 == b
            lhs[kg, b * 64:b * 64 + 32, :] = jnp.where(keep, re, 0.0).astype(jnp.bfloat16)
            lhs[kg, b * 64 + 32:b * 64 + 64, :] = jnp.where(keep, im, 0.0).astype(jnp.bfloat16)
        return 0

    def store_out(p):
        half = pl.ds(p * 32, 32)
        return pltpu.make_async_copy(out_ref.at[:, half], out_hbm.at[:, half], out_sem.at[p])

    def multiply(p, kg):
        right = data[p, :, :, :, kg].reshape(512, CH)
        both = jnp.dot(lhs[p * 8 + kg], right, preferred_element_type=jnp.float32) * scale
        both = both.astype(jnp.bfloat16)
        for b in range(4):
            for ri in range(2):
                out_ref[ri, (p * 8 + kg) * 4 + b] = both[(b * 2 + ri) * 32:(b * 2 + ri + 1) * 32]

    def products(p, fused):
        def step(n, _):
            for j in range(8):
                kg = n * 8 + j
                if fused:
                    build(p * 8 + kg, 0)
                multiply(p, kg)
            return 0

        for h in range(2):
            receive(h, p)
        step(0, 0)
        store_out(p).start()

    @pl.when(z < 8)
    def _():
        products(0, True)
        products(1, True)

    @pl.when(z >= 8)
    def _():
        def build_four(n, _):
            for j in range(4):
                build(n * 4 + j, 0)
            return 0

        lax.fori_loop(0, 4, build_four, 0)
        products(0, False)
        products(1, False)

    cross[0].wait_send()
    cross[1].wait_send()
    for w, d in pairs:
        ref_copy(w, d, q).wait_send()
    for j in range(1, 4):
        far(j, za).wait_send()
    for a in range(4):
        for o in (1, 15, 2 if a < 2 else 14):
            near(o, a, cls).wait_send()
    for h in range(2):
        for p in range(2):
            for i in range(4):
                over_y(h, p, i, q).wait_send()
            for i in range(1, 4):
                over_x(h, p, i, q).wait_send()
    store_out(0).wait()
    store_out(1).wait()


def local(signal, table, window):
    bf16, f32 = jnp.bfloat16, jnp.float32
    dma = pltpu.SemaphoreType.DMA
    return pl.pallas_call(
        kernel,
        out_shape=jax.ShapeDtypeStruct((2, 64, REFS, CH), bf16),
        in_specs=[
            pl.BlockSpec(memory_space=pl.ANY),
            pl.BlockSpec(memory_space=pl.ANY),
            pl.BlockSpec(memory_space=pl.ANY),
        ],
        out_specs=pl.BlockSpec(memory_space=pl.ANY),
        scratch_shapes=[
            pltpu.VMEM((1, L), f32),
            pltpu.VMEM((2, 64, REFS, CH), bf16),
            pltpu.VMEM((CH, SEG_DEV * L), bf16),
            pltpu.VMEM((CH, SEG_DEV * L), bf16),
            pltpu.VMEM((8, 2, 64, L), bf16),
            pltpu.VMEM((2, SEG_DEV, CH, L), bf16),
            pltpu.VMEM((2, 2, 8, 2, 8, 16, CH), bf16),
            pltpu.VMEM((2, 8, 2, 2, 8, 16, CH), bf16),
            pltpu.VMEM((8, 8, 128), f32),
            pltpu.VMEM((2, 8, 8, 128), f32),
            pltpu.VMEM((4, 4, 2, 16, 512), bf16),
            pltpu.VMEM((4, REFS * 16, 128), f32),
            pltpu.VMEM((16, 256, 512), bf16),
            dma, dma, dma((8,)), dma((2,)), dma((2,)), dma((2, 2)),
            *[dma((2, 2, 4)) for _ in range(4)], dma((2, 8)), dma((2, 8)),
            dma((4,)), dma((4,)), dma((4, 4)), dma((4, 4)), dma((2,)), pltpu.SemaphoreType.REGULAR((7,)),
        ],
        compiler_params=pltpu.CompilerParams(
            collective_id=0, has_side_effects=True, vmem_limit_bytes=52 * 2**20
        ),
        cost_estimate=pl.CostEstimate(flops=5 * 10**9, bytes_accessed=8 * 10**6, transcendentals=0),
        name="cross_spectra",
    )(signal, table, window)


def solution(mesh):
    table = make_table()
    window = make_window()[None, :]

    def whole(signal):
        return local(signal, jnp.asarray(table), jnp.asarray(window))

    return jax.shard_map(
        whole, mesh=mesh, in_specs=(P("chan", "freq"),), out_specs=P(None, "freq", None, "chan"), check_vma=False
    )
```
